256 devices in a mesh: seq: 32 (over z, y_lo, core), row: 2 (over y_hi), col: 4 (over x).
Axes of the slice: x: 4, y: 4 (y_hi: 2, y_lo: 2; y = y_hi * 2 + y_lo), z: 8, core: 2. Of those that a mesh axis runs over, the one named last changes fastest.
Arguments:
- activations: bfloat16 [20480, 3072], P('seq', 'col'), may hold values from -8 to 8
- qkv_weight: bfloat16 [3072, 3, 3072], P('col', None, 'row'), may hold values from -1 to 1
- grad_out: bfloat16 [20480, 3072], P('seq', ('row', 'col')), may hold values from -6 to 6
Outputs:
- attention: bfloat16 [20480, 3072], P('seq', ('row', 'col'))
- grad_input: bfloat16 [20480, 3072], P(('seq', 'row'), 'col')
The draws below stay inside these ranges and needn't reach their ends.
All inputs are finite; a program needn't handle non-finite values.
Results may differ from the reference program's by a relative error of at most 0.007.
The reference program's roundings to bfloat16 on the way (of `projections`, `rounded`, `score_grad` and `qkv_grad`) count: a program that leaves them out, or rounds other values in their place, can miss the bound.
Values may be sent and summed in bfloat16 or wider, within the bound.
A program may use at most 128 MiB of HBM per device.

```python
import math
import jax
import jax.numpy as jnp
from jax import lax

D = 3072
HEADS = 24
HEAD = 128
SHARD = 640
TOKENS = 20480
N_SEQ = 32


def draw_activations(key, part):
    key = jax.random.fold_in(key, 3)
    base_key = jax.random.fold_in(key, 0)
    field = jax.random.normal(base_key, (TOKENS, D), jnp.float32)
    return jnp.clip(field, -6.0, 6.0).astype(jnp.bfloat16)


def draw_qkv_weight(key, part):
    key = jax.random.fold_in(key, 7)
    first_key, second_key, third_key = jax.random.split(key, 3)
    shape = (D, HEADS * HEAD)
    first = jnp.clip(jax.random.normal(first_key, shape, jnp.float32), -4.0, 4.0)
    second = jnp.clip(jax.random.normal(second_key, shape, jnp.float32), -4.0, 4.0)
    third = jnp.clip(jax.random.normal(third_key, shape, jnp.float32), -4.0, 4.0)
    stacked = jnp.stack([1.5 * first, 1.5 * second, third], axis=1) / math.sqrt(D)
    return stacked.astype(jnp.bfloat16)


def level_of(stream_key, extent, pieces, smallest, high):
    level = 1.0
    for axis_at, parts in pieces:
        heights = jax.random.uniform(jax.random.fold_in(jax.random.fold_in(stream_key, 6), axis_at), (parts,), jnp.float32, smallest / len(pieces), high / len(pieces))
        level = level * jnp.repeat(jnp.exp(heights), extent[axis_at] // parts).reshape((-1,) + (1,) * (len(extent) - 1 - axis_at))
    return level


def scatter_about(stream_key, shape, deviation, limit, cuts=(), kind=jnp.bfloat16):
    level = level_of(stream_key, shape, cuts, -0.22, 0.18) if cuts else 1.0
    result = jax.random.normal(stream_key, shape, jnp.float32) * deviation * level
    return jnp.minimum(jnp.maximum(result, -limit), limit).astype(kind)


def setup_inputs(seed: int = 0) -> dict:
    key_of = jax.random.split(jax.random.key(seed), 4)
    activations = draw_activations(jax.random.fold_in(key_of[3], 71), 0)
    qkv_weight = draw_qkv_weight(jax.random.fold_in(key_of[3], 71), 0)
    grad_out = scatter_about(key_of[2], (TOKENS, HEADS * HEAD), 1.0, 6.0, ((0, 32), (1, 8)))
    return {"activations": activations, "qkv_weight": qkv_weight, "grad_out": grad_out}


def attend(query, keys, values, prior_keys, prior_values, upstream, has_prior):
    length = query.shape[0]
    scaling = HEAD ** -0.5
    query_wide = query.astype(jnp.float32)
    all_keys = jnp.concatenate([prior_keys, keys], 0).astype(jnp.float32)
    all_values = jnp.concatenate([prior_values, values], 0).astype(jnp.float32)
    upstream_wide = upstream.astype(jnp.float32)
    scores = jnp.einsum("qhe,khe->hqk", query_wide, all_keys) * scaling
    position = jnp.arange(length, dtype=jnp.int32)
    causal = position[:, None] >= position[None, :]
    visible = jnp.concatenate([jnp.broadcast_to(has_prior, (length, length)), causal], 1)
    scores = jnp.where(visible[None], scores, -jnp.inf)
    highest = jnp.max(scores, axis=2, keepdims=True)
    raised = jnp.exp(scores - highest)
    weights = raised / jnp.sum(raised, axis=2, keepdims=True)
    rounded = lax.optimization_barrier(weights.astype(jnp.bfloat16)).astype(jnp.float32)
    context = jnp.einsum("hqk,khe->qhe", rounded, all_values)
    value_grad = jnp.einsum("hqk,qhe->khe", rounded, upstream_wide)
    prob_grad = jnp.einsum("qhe,khe->hqk", upstream_wide, all_values)
    row_delta = jnp.transpose(jnp.sum(upstream_wide * context, axis=2))[:, :, None]
    score_grad = lax.optimization_barrier((weights * (prob_grad - row_delta)).astype(jnp.bfloat16)).astype(jnp.float32)
    query_grad = jnp.einsum("hqk,khe->qhe", score_grad, all_keys) * scaling
    key_grad = jnp.einsum("hqk,qhe->khe", score_grad, query_wide) * scaling
    return (context.astype(jnp.bfloat16), query_grad, key_grad[:length], key_grad[length:],
            value_grad[:length], value_grad[length:])


def shard_step(items):
    return attend(*items)


def reference(activations, qkv_weight, grad_out):
    head_width = HEADS * HEAD
    columns = qkv_weight.reshape(D, 3 * head_width)
    projections = lax.optimization_barrier(
        jnp.dot(activations, columns, preferred_element_type=jnp.float32).astype(jnp.bfloat16))
    blocks = projections.reshape(N_SEQ, SHARD, 3, HEADS, HEAD)
    upstream = grad_out.reshape(N_SEQ, SHARD, HEADS, HEAD)
    keys = blocks[:, :, 1]
    values = blocks[:, :, 2]
    prior_keys = jnp.concatenate([jnp.zeros_like(keys[:1]), keys[:-1]], 0)
    prior_values = jnp.concatenate([jnp.zeros_like(values[:1]), values[:-1]], 0)
    has_prior = jnp.arange(N_SEQ, dtype=jnp.int32) > 0
    context, query_grad, key_prior, key_own, value_prior, value_own = lax.map(
        shard_step, (blocks[:, :, 0], keys, values, prior_keys, prior_values, upstream, has_prior))
    key_total = key_own + jnp.concatenate([key_prior[1:], jnp.zeros_like(key_prior[:1])], 0)
    value_total = value_own + jnp.concatenate([value_prior[1:], jnp.zeros_like(value_prior[:1])], 0)
    qkv_grad = jnp.stack([query_grad, key_total, value_total], axis=2).astype(jnp.bfloat16)
    qkv_grad = qkv_grad.reshape(N_SEQ * SHARD, 3 * head_width)
    grad_input = jnp.dot(qkv_grad, columns.T, preferred_element_type=jnp.float32).astype(jnp.bfloat16)
    return context.reshape(N_SEQ * SHARD, head_width), grad_input
```

```python
import functools

import jax
import jax.numpy as jnp
from jax import lax
from jax.experimental import pallas as pl
from jax.experimental.pallas import tpu as pltpu
from jax.sharding import PartitionSpec as P

HEAD = 128
HEADS = 3
LOG2E = 1.4426950408889634
MESH = pl.DeviceIdType.MESH
BF = jnp.bfloat16
F32 = jnp.float32
PLACE = (2, 0, 1)


def dot(a, b):
    return jnp.dot(a, b, preferred_element_type=F32)


def dot_nt(a, b):
    return lax.dot_general(a, b, (((1,), (1,)), ((), ())), preferred_element_type=F32)


def kernel(
    act_hbm, w_hbm, go_hbm, attn_ref, gin_ref,
    act, w, acc, go, go_t, query, pair, pair_t, prior, prior_t, own_grad, prior_grad,
    sent_grad, back_grad, grads, opp_out, opp_in, full_out, full_in, row_out, row_in,
    local_sem, inj_send, inj_recv, act_send, act_recv, z_send, z_recv, core_send, core_recv,
    kv_send, kv_recv, gr_send, gr_recv, opp_send, opp_recv, full_send, full_recv, row_send, row_recv,
):
    seq, row, col = lax.axis_index("seq"), lax.axis_index("row"), lax.axis_index("col")
    n_seq = lax.axis_size("seq")
    n_z = n_seq // 4
    z, core = seq // 4, seq % 2
    length, depth = act_hbm.shape
    width = go_hbm.shape[1]
    half = length // 2
    part = depth // (2 * n_z)

    def at_col(step):
        return (seq, row, (col + step) % 4)

    def at_seq(index):
        return (index, row, col)

    right, opposite, left = at_col(1), at_col(2), at_col(3)
    up, down = at_seq((seq + 4) % n_seq), at_seq((seq + n_seq - 4) % n_seq)
    twin = at_seq(seq + 1 - 2 * core)
    following, previous = at_seq((seq + 1) % n_seq), at_seq((seq + n_seq - 1) % n_seq)
    partner = (seq, 1 - row, col)

    def remote(src, dst, send, recv, device):
        return pltpu.make_async_remote_copy(
            src_ref=src, dst_ref=dst, send_sem=send, recv_sem=recv, device_id=device, device_id_type=MESH
        )

    own_cols = pl.ds(pl.multiple_of(col * width, 128), width)
    locals_ = [pltpu.make_async_copy(act_hbm, act.at[0], local_sem.at[0])]
    for kind in range(3):
        at = PLACE[kind] * width
        locals_.append(
            pltpu.make_async_copy(w_hbm.at[kind, :, own_cols], w.at[0, :, at : at + width], local_sem.at[1 + kind])
        )
    for head in range(HEADS):
        locals_.append(
            pltpu.make_async_copy(
                go_hbm.at[:, head * HEAD : (head + 1) * HEAD], go.at[head], local_sem.at[4 + head]
            )
        )
    for copy in locals_:
        copy.start()

    barrier = pltpu.get_barrier_semaphore()
    friends = (right, opposite, left, up, down, twin, following, previous, partner)
    for friend in friends:
        pl.semaphore_signal(barrier, inc=1, device_id=friend, device_id_type=MESH)
    pl.semaphore_wait(barrier, len(friends))

    def rows_of(z_at, core_at):
        return pl.ds(pl.multiple_of(z_at * (2 * part) + core_at * part, 16), part)

    mine = rows_of(z, core)
    injections = []
    for step in (2, 1, 3):
        cols = pl.ds(pl.multiple_of(((col + step) % 4) * width, 128), width)
        for kind in range(3):
            at = PLACE[kind] * width
            injections.append(
                remote(
                    w_hbm.at[kind, mine, cols],
                    w.at[4 - step, mine, at : at + width],
                    inj_send.at[4 - step, kind],
                    inj_recv.at[4 - step, kind],
                    at_col(step),
                )
            )
    for copy in injections:
        copy.start()

    top, bottom = pl.ds(0, half), pl.ds(half, half)
    act_copies = [
        remote(act_hbm.at[top], act.at[3, top], act_send.at[0], act_recv.at[0], right),
        remote(act_hbm.at[bottom], act.at[1, bottom], act_send.at[1], act_recv.at[1], left),
        remote(act_hbm.at[bottom], act.at[3, bottom], act_send.at[2], act_recv.at[2], right),
        remote(act_hbm.at[top], act.at[1, top], act_send.at[3], act_recv.at[3], left),
        remote(act.at[3, top], act.at[2, top], act_send.at[4], act_recv.at[4], right),
        remote(act.at[1, bottom], act.at[2, bottom], act_send.at[5], act_recv.at[5], left),
    ]
    for copy in act_copies[:4]:
        copy.start()

    for copy in locals_[:4]:
        copy.wait()

    def project(index, first):
        @pl.loop(0, 2)
        def _(i):
            rows = pl.ds(pl.multiple_of(i * half, half), half)
            term = dot(act[index, rows, :], w[index])
            acc[rows, :] = term if first else acc[rows, :] + term

    project(0, True)
    for copy in locals_[4:]:
        copy.wait()
    for head in range(HEADS):
        go_t[head] = jnp.transpose(go[head])

    for copy in injections:
        copy.wait_recv()
    cut = 640
    total = 3 * width

    def ring(way, step):
        origin = (z + n_z - step) % n_z if way == 0 else (z + step) % n_z
        rows = rows_of(origin, core)
        if step < n_z // 2 - 1:
            block = w.at[1:4, rows, :]
        else:
            block = w.at[1:4, rows, 0:cut] if way == 0 else w.at[1:4, rows, cut:total]
        return remote(block, block, z_send.at[way, step], z_recv.at[way, step], (up, down)[way])

    def across(index, origin):
        block = w.at[1:4, rows_of(origin, core), :]
        return remote(block, block, core_send.at[index], core_recv.at[index], twin)

    steps = n_z // 2
    rings = [[ring(way, step) for way in (0, 1)] for step in range(steps)]
    acrosses = [across(0, z)]
    for step in range(1, steps):
        acrosses.append(across(2 * step - 1, (z + n_z - step) % n_z))
        acrosses.append(across(2 * step, (z + step) % n_z))
    acrosses.append(across(2 * steps - 1, (z + steps) % n_z))
    for copy in rings[0]:
        copy.start()
    acrosses[0].start()
    for step in range(1, steps):
        for way in (0, 1):
            rings[step - 1][way].wait_recv()
            rings[step][way].start()
            acrosses[2 * step - 1 + way].start()
        if step == 1:
            for i in (0, 1):
                act_copies[i].wait_recv()
                act_copies[4 + i].start()
    for way in (0, 1):
        rings[steps - 1][way].wait_recv()
    acrosses[-1].start()
    for copy in acrosses:
        copy.wait_recv()
    for i in (2, 3):
        act_copies[i].wait_recv()
    project(1, False)
    project(3, False)
    for i in (4, 5):
        act_copies[i].wait_recv()

    for i in range(2):
        rows = pl.ds(i * half, half)
        done = (acc[rows, 0 : 2 * width] + dot(act[2, rows, :], w[2, :, 0 : 2 * width])).astype(BF)
        for head in range(HEADS):
            for kind in range(2):
                at = kind * width + head * HEAD
                pair[head, kind, rows, :] = done[:, at : at + HEAD]
    kv_copies = [
        remote(pair.at[head], prior.at[head], kv_send.at[head], kv_recv.at[head], following) for head in range(HEADS)
    ]
    for copy in kv_copies:
        copy.start()
    for i in range(2):
        rows = pl.ds(i * half, half)
        done = (acc[rows, 2 * width : total] + dot(act[2, rows, :], w[2, :, 2 * width : total])).astype(BF)
        for head in range(HEADS):
            query[head, rows, :] = done[:, head * HEAD : (head + 1) * HEAD]
    for head in range(HEADS):
        for kind in range(2):
            pair_t[head, kind] = jnp.transpose(pair[head, kind])

    scaling = HEAD**-0.5
    base = scaling * LOG2E
    has_prior = seq > 0

    gr_copies = [
        remote(sent_grad.at[head], back_grad.at[head], gr_send.at[head], gr_recv.at[head], previous)
        for head in range(HEADS)
    ]

    for head in range(HEADS):
        kv_copies[head].wait_recv()
        for kind in range(2):
            prior_t[kind] = jnp.transpose(prior[head, kind])
        prior_keys, prior_values = prior[head, 0], prior[head, 1]
        for q0, size in ((0, 256), (256, 256), (512, 128)):
            seen = q0 + size
            q_t = query[head, q0:seen, :]
            up_q = go[head, q0:seen, :]
            s_own = dot_nt(pair[head, 0, 0:seen, :], q_t)
            s_prior = dot_nt(prior_keys, q_t)
            key_at = lax.broadcasted_iota(jnp.int32, (seen, size), 0)
            query_at = lax.broadcasted_iota(jnp.int32, (seen, size), 1) + q0
            s_own = jnp.where(key_at <= query_at, s_own, -jnp.inf)
            top_prior = jnp.where(has_prior, jnp.max(s_prior, axis=0, keepdims=True), -jnp.inf)
            highest = jnp.maximum(jnp.max(s_own, axis=0, keepdims=True), top_prior) * base
            e_own = jnp.exp2(s_own * base - highest)
            e_prior = jnp.exp2(s_prior * base - jnp.where(has_prior, highest, jnp.inf))
            inverse = 1.0 / (jnp.sum(e_own, axis=0, keepdims=True) + jnp.sum(e_prior, axis=0, keepdims=True))
            w_own, w_prior = e_own * inverse, e_prior * inverse
            p_own, p_prior = w_own.astype(BF), w_prior.astype(BF)
            ctx_t = dot(prior_t[1], p_prior) + dot(pair_t[head, 1, :, 0:seen], p_own)
            delta = jnp.sum(go_t[head, :, q0:seen].astype(F32) * ctx_t, axis=0, keepdims=True)
            attn_ref[q0:seen, head * HEAD : (head + 1) * HEAD] = jnp.transpose(ctx_t).astype(BF)
            ds_own = (w_own * (dot_nt(pair[head, 1, 0:seen, :], up_q) - delta)).astype(BF)
            ds_prior = (w_prior * (dot_nt(prior_values, up_q) - delta)).astype(BF)
            dq_t = dot(prior_t[0], ds_prior) + dot(pair_t[head, 0, :, 0:seen], ds_own)
            at = 2 * width + head * HEAD
            grads[q0:seen, at : at + HEAD] = (jnp.transpose(dq_t) * scaling).astype(BF)
            terms = (dot(ds_own, q_t), dot(p_own, up_q))
            prior_terms = (dot(ds_prior, q_t), dot(p_prior, up_q))
            for kind in range(2):
                if q0:
                    own_grad[head, kind, 0:q0, :] = own_grad[head, kind, 0:q0, :] + terms[kind][0:q0]
                    prior_grad[kind] = prior_grad[kind] + prior_terms[kind]
                else:
                    prior_grad[kind] = prior_terms[kind]
                own_grad[head, kind, q0:seen, :] = terms[kind][q0:seen]
        sent_grad[head, 0] = (prior_grad[0] * scaling).astype(BF)
        sent_grad[head, 1] = prior_grad[1].astype(BF)
        gr_copies[head].start()

    for head in range(HEADS):
        gr_copies[head].wait_recv()
        for kind in range(2):
            at = kind * width + head * HEAD
            own = own_grad[head, kind]
            own = own * scaling if kind == 0 else own
            grads[:, at : at + HEAD] = (own + back_grad[head, kind].astype(F32)).astype(BF)

    halves = [pl.ds(pl.multiple_of((1 - row) * half, half), half), pl.ds(pl.multiple_of(row * half, half), half)]
    mid = depth // 2

    def share(index, which):
        return dot_nt(grads[halves[which], :], w[index])

    opp_copies, full_copies = [], []
    for which in (0, 1):
        for way in (0, 1):
            opp_copies.append(
                remote(
                    opp_out.at[way, which], opp_in.at[way, which], opp_send.at[way, which], opp_recv.at[way, which],
                    (right, left)[way],
                )
            )
            full_copies.append(
                remote(
                    full_out.at[way, which], full_in.at[way, which], full_send.at[way, which],
                    full_recv.at[way, which], (right, left)[way],
                )
            )
    for which in (0, 1):
        term = share(2, which).astype(BF)
        opp_out[0, which] = term[:, mid:]
        opp_out[1, which] = term[:, :mid]
        for way in (0, 1):
            opp_copies[2 * which + way].start()
    for which in (0, 1):
        for way in (0, 1):
            term = share((1, 3)[way], which)
            opp_copies[2 * which + way].wait_recv()
            arrived = opp_in[way, which].astype(F32)
            if way == 0:
                full_out[way, which, :, :mid] = term[:, :mid].astype(BF)
                full_out[way, which, :, mid:] = (term[:, mid:] + arrived).astype(BF)
            else:
                full_out[way, which, :, :mid] = (term[:, :mid] + arrived).astype(BF)
                full_out[way, which, :, mid:] = term[:, mid:].astype(BF)
            full_copies[2 * which + way].start()
    row_copy = remote(row_out, row_in, row_send, row_recv, partner)
    for which in (0, 1):
        term = share(0, which)
        for way in (0, 1):
            full_copies[2 * which + way].wait_recv()
            term = term + full_in[way, which].astype(F32)
        if which == 0:
            row_out[...] = term.astype(BF)
            row_copy.start()
        else:
            row_copy.wait_recv()
            gin_ref[...] = (term + row_in[...].astype(F32)).astype(BF)

    for copy in injections + act_copies + [c for pair_ in rings for c in pair_] + acrosses:
        copy.wait_send()
    for copy in kv_copies + gr_copies + opp_copies + full_copies + [row_copy]:
        copy.wait_send()


def on_device(activations, qkv_weight, grad_out):
    length, depth = activations.shape
    width = grad_out.shape[1]
    half = length // 2
    steps = lax.axis_size("seq") // 8
    weights = jnp.transpose(qkv_weight, (1, 0, 2))
    anywhere = pl.BlockSpec(memory_space=pl.ANY)
    vmem = pl.BlockSpec(memory_space=pltpu.VMEM)
    dma = pltpu.SemaphoreType.DMA
    return pl.pallas_call(
        kernel,
        out_shape=(
            jax.ShapeDtypeStruct((length, width), BF),
            jax.ShapeDtypeStruct((half, depth), BF),
        ),
        in_specs=[anywhere] * 3,
        out_specs=(vmem, vmem),
        scratch_shapes=[
            pltpu.VMEM((4, length, depth), BF),
            pltpu.VMEM((4, depth, 3 * width), BF),
            pltpu.VMEM((length, 3 * width), F32),
            pltpu.VMEM((HEADS, length, HEAD), BF),
            pltpu.VMEM((HEADS, HEAD, length), BF),
            pltpu.VMEM((HEADS, length, HEAD), BF),
            pltpu.VMEM((HEADS, 2, length, HEAD), BF),
            pltpu.VMEM((HEADS, 2, HEAD, length), BF),
            pltpu.VMEM((HEADS, 2, length, HEAD), BF),
            pltpu.VMEM((2, HEAD, length), BF),
            pltpu.VMEM((HEADS, 2, length, HEAD), F32),
            pltpu.VMEM((2, length, HEAD), F32),
            pltpu.VMEM((HEADS, 2, length, HEAD), BF),
            pltpu.VMEM((HEADS, 2, length, HEAD), BF),
            pltpu.VMEM((length, 3 * width), BF),
            pltpu.VMEM((2, 2, half, depth // 2), BF),
            pltpu.VMEM((2, 2, half, depth // 2), BF),
            pltpu.VMEM((2, 2, half, depth), BF),
            pltpu.VMEM((2, 2, half, depth), BF),
            pltpu.VMEM((half, depth), BF),
            pltpu.VMEM((half, depth), BF),
            dma((7,)),
            dma((4, 3)),
            dma((4, 3)),
            dma((6,)),
            dma((6,)),
            dma((2, steps)),
            dma((2, steps)),
            dma((2 * steps,)),
            dma((2 * steps,)),
            dma((HEADS,)),
            dma((HEADS,)),
            dma((HEADS,)),
            dma((HEADS,)),
            dma((2, 2)),
            dma((2, 2)),
            dma((2, 2)),
            dma((2, 2)),
            dma,
            dma,
        ],
        compiler_params=pltpu.CompilerParams(
            collective_id=0, has_side_effects=True, vmem_limit_bytes=60 * 2**20
        ),
    )(activations, weights, grad_out)


def solution(mesh):
    in_specs = (P("seq", "col"), P("col", None, "row"), P("seq", ("row", "col")))
    out_specs = (P("seq", ("row", "col")), P(("seq", "row"), "col"))
    return jax.shard_map(on_device, mesh=mesh, in_specs=in_specs, out_specs=out_specs, check_vma=False)
```

```python
import functools

import jax
import jax.numpy as jnp
from jax import lax
from jax.experimental import pallas as pl
from jax.experimental.pallas import tpu as pltpu
from jax.sharding import PartitionSpec as P

HEAD = 128
HEADS = 3
GROUPS = 4
TILES = ((256, 256), (512, 256), (640, 128))
LOG2E = 1.4426950408889634
MESH = pl.DeviceIdType.MESH
BF = jnp.bfloat16
F32 = jnp.float32
PLACE = (2, 0, 1)


def dot(a, b):
    return jnp.dot(a, b, preferred_element_type=F32)


def dot_nt(a, b):
    return lax.dot_general(a, b, (((1,), (1,)), ((), ())), preferred_element_type=F32)


def kernel(
    act_hbm, w_hbm, go_hbm, attn_ref, gin_ref,
    act, w, acc, go, go_t, query, pair, pair_t, prior, prior_t,
    s_a, s_b, s_c, dp_a, dp_b, dp_c, p_a, p_b, p_c, ds_a, ds_b, ds_c, p_prior, ds_prior,
    own_grad, sent_grad, back_grad, grads, cross_out, cross_in, opp_out, opp_in, full_out, full_in, row_out, row_in,
    local_sem, inj_send, inj_recv, act_send, act_recv, fwd_send, fwd_recv, swap_send, swap_recv,
    z_send, z_recv, y_send, y_recv, core_send, core_recv, kv_send, kv_recv, gr_send, gr_recv,
    cross_send, cross_recv, opp_send, opp_recv, full_send, full_recv, row_send, row_recv,
):
    seq, row, col = lax.axis_index("seq"), lax.axis_index("row"), lax.axis_index("col")
    n_seq = lax.axis_size("seq")
    n_z = n_seq // 4
    z, side, core = seq // 4, (seq // 2) % 2, seq % 2
    length, depth = act_hbm.shape
    width = go_hbm.shape[1]
    total = 3 * width
    half = length // 2
    group = length // GROUPS
    part = depth // (2 * n_z)

    def at_col(step):
        return (seq, row, (col + step) % 4)

    def at_seq(index):
        return (index, row, col)

    right, opposite, left = at_col(1), at_col(2), at_col(3)
    up, down = at_seq((seq + 4) % n_seq), at_seq((seq + n_seq - 4) % n_seq)
    twin = at_seq(seq + 1 - 2 * core)
    beside = at_seq(seq + 2 - 4 * side)
    following, previous = at_seq((seq + 1) % n_seq), at_seq((seq + n_seq - 1) % n_seq)
    partner = (seq, 1 - row, col)
    sent = []

    def remote(src, dst, send, recv, device):
        return pltpu.make_async_remote_copy(
            src_ref=src, dst_ref=dst, send_sem=send, recv_sem=recv, device_id=device, device_id_type=MESH
        )

    def start(copy):
        copy.start()
        sent.append(copy)

    own_cols = pl.ds(pl.multiple_of(col * width, 128), width)
    locals_ = [pltpu.make_async_copy(act_hbm, act.at[0], local_sem.at[0])]
    for kind in range(3):
        at = PLACE[kind] * width
        locals_.append(
            pltpu.make_async_copy(w_hbm.at[kind, :, own_cols], w.at[0, :, at : at + width], local_sem.at[1 + kind])
        )
    for head in range(HEADS):
        locals_.append(
            pltpu.make_async_copy(
                go_hbm.at[:, head * HEAD : (head + 1) * HEAD], go.at[head], local_sem.at[4 + head]
            )
        )
    for copy in locals_:
        copy.start()

    barrier = pltpu.get_barrier_semaphore()
    friends = (right, opposite, left, up, down, twin, beside, following, previous, partner)
    for friend in friends:
        pl.semaphore_signal(barrier, inc=1, device_id=friend, device_id_type=MESH)
    pl.semaphore_wait(barrier, len(friends))

    def rows_of(z_at, core_at):
        return pl.ds(pl.multiple_of(z_at * (2 * part) + core_at * part, 16), part)

    mine = rows_of(z, core)
    only = 1 + 2 * side

    def inject(index, kind, step):
        cols = pl.ds(pl.multiple_of(((col + step) % 4) * width, 128), width)
        at = PLACE[kind] * width
        return remote(
            w_hbm.at[kind, mine, cols], w.at[4 - step, mine, at : at + width],
            inj_send.at[index], inj_recv.at[index], at_col(step),
        )

    pair_injections = [
        inject(index, kind, step)
        for index, (kind, step) in enumerate(((1, 2), (2, 2), (1, 4 - only), (2, 4 - only)))
    ]
    query_injections = [inject(4 + index, 0, step) for index, step in enumerate((2, 1, 3))]

    early_at, late_at = row * half, (1 - row) * half
    early, late = (pl.ds(pl.multiple_of(at, 64), half) for at in (early_at, late_at))
    quarters = [pl.ds(pl.multiple_of(early_at + i * group, 32), group) for i in (0, 1)]

    def own_act(index, way):
        rows = (quarters[way], quarters[1 - way], late)[index]
        return remote(
            act_hbm.at[rows], act.at[3 - 2 * way, rows], act_send.at[way, index], act_recv.at[way, index],
            (right, left)[way],
        )

    def far_act(way):
        rows = quarters[way]
        there = act.at[2, rows]
        return (
            remote(act.at[3 - 2 * way, rows], there, fwd_send.at[way], fwd_recv.at[way], (right, left)[way]),
            remote(there, there, swap_send.at[way], swap_recv.at[way], partner),
        )

    own_acts = [[own_act(index, way) for way in (0, 1)] for index in range(3)]
    far_acts = [far_act(way) for way in (0, 1)]
    for copy in pair_injections + own_acts[0] + query_injections:
        start(copy)

    def pass_on():
        for way in (0, 1):
            own_acts[0][way].wait_recv()
            start(far_acts[way][0])
        for copies in own_acts[1:]:
            for copy in copies:
                start(copy)

    def hand_over():
        for copy, swap in far_acts:
            copy.wait_recv()
            start(swap)

    for copy in locals_[:4]:
        copy.wait()

    @pl.loop(0, 2)
    def _(i):
        rows = pl.ds(pl.multiple_of(i * half, half), half)
        acc[rows, :] = dot(act[0, rows, :], w[0])

    for copy in locals_[4:]:
        copy.wait()
    for head in range(HEADS):
        go_t[head] = jnp.transpose(go[head])

    def ring(way, step):
        origin = (z + n_z - step) % n_z if way == 0 else (z + step) % n_z
        rows = rows_of(origin, core)
        if step < n_z // 2 - 1:
            blocks = [w.at[pl.ds(1 + side, 2), rows, 0 : 2 * width], w.at[1:4, rows, 2 * width : total]]
        elif way == 0:
            blocks = [w.at[2, rows, 0 : 2 * width], w.at[1:3, rows, 2 * width : total]]
        else:
            blocks = [w.at[only, rows, 0 : 2 * width], w.at[3, rows, 2 * width : total]]
        return [
            remote(block, block, z_send.at[way, step, i], z_recv.at[way, step, i], (up, down)[way])
            for i, block in enumerate(blocks)
        ]

    steps = n_z // 2
    origins = [[z]]
    for step in range(1, steps):
        origins.append([(z + n_z - step) % n_z, (z + step) % n_z])
    origins.append([(z + steps) % n_z])

    def spread(index, origin):
        rows = rows_of(origin, core)
        blocks = (w.at[only, rows, 0 : 2 * width], w.at[1:4, rows, 0 : 2 * width], w.at[1:4, rows, 2 * width : total])
        return (
            remote(blocks[0], blocks[0], y_send.at[index], y_recv.at[index], beside),
            remote(blocks[1], blocks[1], core_send.at[0, index], core_recv.at[0, index], twin),
            remote(blocks[2], blocks[2], core_send.at[1, index], core_recv.at[1, index], twin),
        )

    rings = [[ring(way, step) for way in (0, 1)] for step in range(steps)]
    spreads, count = [], 0
    for members in origins:
        spreads.append([spread(count + i, origin) for i, origin in enumerate(members)])
        count += len(members)

    def across_pairs(step):
        for exchange, across, _ in spreads[step]:
            exchange.wait_recv()
            start(across)

    def turn_pairs(step):
        for way in (0, 1):
            if step > 0:
                rings[step - 1][way][0].wait_recv()
            if step < steps:
                start(rings[step][way][0])
                if way < len(spreads[step]):
                    start(spreads[step][way][0])
        if step == steps:
            start(spreads[step][0][0])
        if step > 0:
            across_pairs(step - 1)

    def turn_queries(step):
        for way in (0, 1):
            if step > 0:
                rings[step - 1][way][1].wait_recv()
            if step < steps:
                start(rings[step][way][1])
        for _, _, across in spreads[step]:
            start(across)

    for copy in pair_injections:
        copy.wait_recv()
    turn_pairs(0)
    turn_pairs(1)
    for copy in query_injections:
        copy.wait_recv()
    turn_queries(0)
    pass_on()
    turn_pairs(2)
    turn_queries(1)
    hand_over()
    turn_pairs(3)
    turn_queries(2)
    turn_pairs(4)
    across_pairs(steps)
    turn_queries(3)
    for members in spreads:
        for _, across, _ in members:
            across.wait_recv()

    def keep_pairs(rows, done):
        for head in range(HEADS):
            for kind in range(2):
                at = kind * width + head * HEAD
                pair[head, kind, rows, :] = done[:, at : at + HEAD].astype(BF)

    def keep_queries(rows, done):
        for head in range(HEADS):
            query[head, rows, :] = done[:, head * HEAD : (head + 1) * HEAD].astype(BF)

    def kv_copy(index, heads, rows):
        return remote(
            pair.at[heads, :, rows, :], prior.at[heads, :, rows, :], kv_send.at[index], kv_recv.at[index], following
        )

    kv_copies = [kv_copy(HEADS, pl.ds(0, HEADS), early)]
    kv_copies += [kv_copy(head, pl.ds(head, 1), late) for head in range(HEADS)]
    for copy in own_acts[1]:
        copy.wait_recv()

    def product(rows, cols):
        return acc[rows, cols] + sum(dot(act[index, rows, :], w[index, :, cols]) for index in (1, 2, 3))

    pair_cols, query_cols = pl.ds(0, 2 * width), pl.ds(2 * width, width)
    keep_pairs(early, product(early, pair_cols))
    start(kv_copies[0])
    turn_queries(4)
    for members in spreads:
        for _, _, across in members:
            across.wait_recv()
    keep_queries(early, product(early, query_cols))
    for copy in own_acts[2]:
        copy.wait_recv()
    for _, swap in far_acts:
        swap.wait_recv()
    keep_pairs(late, product(late, pair_cols))
    for copy in kv_copies[1:]:
        start(copy)
    keep_queries(late, product(late, query_cols))
    for head in range(HEADS):
        for kind in range(2):
            pair_t[head, kind] = jnp.transpose(pair[head, kind])

    scaling = HEAD**-0.5
    base = scaling * LOG2E
    has_prior = seq > 0
    tiles = (
        (0, 256, s_a, dp_a, p_a, ds_a),
        (256, 256, s_b, dp_b, p_b, ds_b),
        (512, 128, s_c, dp_c, p_c, ds_c),
    )
    for head in range(HEADS):
        for q0, size, s_own, dp_own, _, _ in tiles:
            seen = q0 + size
            scores = dot_nt(pair[head, 0, 0:seen, :], query[head, q0:seen, :])
            key_at = lax.broadcasted_iota(jnp.int32, (seen, size), 0)
            query_at = lax.broadcasted_iota(jnp.int32, (seen, size), 1) + q0
            s_own[head] = jnp.where(key_at <= query_at, scores, -jnp.inf)
            dp_own[head] = dot_nt(pair[head, 1, 0:seen, :], go[head, q0:seen, :])

    order = [
        pl.ds(pl.multiple_of(at * half + i * group, 32), group) for at in (1 - row, row) for i in range(GROUPS // 2)
    ]
    gr_copies = [
        remote(sent_grad.at[head], back_grad.at[head], gr_send.at[head], gr_recv.at[head], previous)
        for head in range(HEADS - 1)
    ]
    gr_copies += [
        remote(
            sent_grad.at[HEADS - 1, :, rows, :], back_grad.at[HEADS - 1, :, rows, :],
            gr_send.at[HEADS - 1 + i], gr_recv.at[HEADS - 1 + i], previous,
        )
        for i, rows in enumerate(order)
    ]
    for head in range(HEADS):
        if head == 0:
            kv_copies[0].wait_recv()
        kv_copies[1 + head].wait_recv()
        for kind in range(2):
            prior_t[head, kind] = jnp.transpose(prior[head, kind])
        for q0, size, s_own, dp_own, p_own, ds_own in tiles:
            seen = q0 + size
            s_prior = dot_nt(prior[head, 0], query[head, q0:seen, :])
            mine_s = s_own[head]
            top_prior = jnp.where(has_prior, jnp.max(s_prior, axis=0, keepdims=True), -jnp.inf)
            highest = jnp.maximum(jnp.max(mine_s, axis=0, keepdims=True), top_prior) * base
            e_own = jnp.exp2(mine_s * base - highest)
            e_prior = jnp.exp2(s_prior * base - jnp.where(has_prior, highest, jnp.inf))
            inverse = 1.0 / (jnp.sum(e_own, axis=0, keepdims=True) + jnp.sum(e_prior, axis=0, keepdims=True))
            w_own, w_prior = e_own * inverse, e_prior * inverse
            b_own, b_prior = w_own.astype(BF), w_prior.astype(BF)
            p_own[head] = b_own
            p_prior[:, q0:seen] = b_prior
            ctx_t = dot(prior_t[head, 1], b_prior) + dot(pair_t[head, 1, :, 0:seen], b_own)
            delta = jnp.sum(go_t[head, :, q0:seen].astype(F32) * ctx_t, axis=0, keepdims=True)
            attn_ref[q0:seen, head * HEAD : (head + 1) * HEAD] = jnp.transpose(ctx_t).astype(BF)
            ds_own[head] = (w_own * (dp_own[head] - delta)).astype(BF)
            dp_prior = dot_nt(prior[head, 1], go[head, q0:seen, :])
            ds_prior[head, :, q0:seen] = (w_prior * (dp_prior - delta)).astype(BF)
        if head < HEADS - 1:
            sent_grad[head, 0] = (dot(ds_prior[head], query[head]) * scaling).astype(BF)
            sent_grad[head, 1] = dot(p_prior[...], go[head]).astype(BF)
            start(gr_copies[head])
        else:
            for i, rows in enumerate(order):
                sent_grad[head, 0, rows, :] = (dot(ds_prior[head, rows, :], query[head]) * scaling).astype(BF)
                sent_grad[head, 1, rows, :] = dot(p_prior[rows, :], go[head]).astype(BF)
                start(gr_copies[head + i])

    for head in range(HEADS):
        for q0, size, _, _, p_own, ds_own in tiles:
            seen = q0 + size
            dq_t = dot(prior_t[head, 0], ds_prior[head, :, q0:seen]) + dot(pair_t[head, 0, :, 0:seen], ds_own[head])
            at = 2 * width + head * HEAD
            grads[q0:seen, at : at + HEAD] = (jnp.transpose(dq_t) * scaling).astype(BF)
            terms = (dot(ds_own[head], query[head, q0:seen, :]) * scaling, dot(p_own[head], go[head, q0:seen, :]))
            for kind in range(2):
                if q0:
                    own_grad[head, kind, 0:q0, :] = own_grad[head, kind, 0:q0, :] + terms[kind][0:q0]
                own_grad[head, kind, q0:seen, :] = terms[kind][q0:seen]

    mid = depth // 2
    halves = [pl.ds(pl.multiple_of(at * half, half), half) for at in (1 - row, row)]
    pieces = [pl.ds(i * group, group) for i in range(GROUPS // 2)]

    def collect(which):
        if which == 0:
            for head in range(HEADS - 1):
                gr_copies[head].wait_recv()
        for i in range(GROUPS // 2):
            gr_copies[HEADS - 1 + which * (GROUPS // 2) + i].wait_recv()
        rows = halves[which]
        for head in range(HEADS):
            for kind in range(2):
                at = kind * width + head * HEAD
                back = back_grad[head, kind, rows, :].astype(F32)
                grads[rows, at : at + HEAD] = (own_grad[head, kind, rows, :] + back).astype(BF)

    def share(index, which):
        return dot_nt(grads[halves[which], :], w[index])

    cross_copies = [
        remote(cross_out.at[rows], cross_in.at[rows], cross_send.at[i], cross_recv.at[i], partner)
        for i, rows in enumerate(pieces)
    ]
    row_copies = [
        remote(row_out.at[rows], row_in.at[rows], row_send.at[i], row_recv.at[i], partner)
        for i, rows in enumerate(pieces)
    ]
    opp_copies = [
        [
            remote(opp_out.at[way, rows], opp_in.at[way, rows], opp_send.at[way, i], opp_recv.at[way, i], (right, left)[way])
            for i, rows in enumerate(pieces)
        ]
        for way in (0, 1)
    ]
    full_copies = [
        [
            [
                remote(
                    full_out.at[way, which, rows], full_in.at[way, which, rows],
                    full_send.at[way, which, i], full_recv.at[way, which, i], (right, left)[way],
                )
                for i, rows in enumerate(pieces)
            ]
            for which in (0, 1)
        ]
        for way in (0, 1)
    ]

    collect(0)
    for way in (0, 1):
        full_out[way, 0] = share((1, 3)[way], 0).astype(BF)
        for copy in full_copies[way][0]:
            start(copy)
    cross_out[...] = share(2, 0).astype(BF)
    for copy in cross_copies:
        start(copy)
    collect(1)
    term = share(2, 1)
    for i, rows in enumerate(pieces):
        cross_copies[i].wait_recv()
        summed = (term[i * group : (i + 1) * group] + cross_in[rows, :].astype(F32)).astype(BF)
        opp_out[0, rows, :] = summed[:, mid:]
        opp_out[1, rows, :] = summed[:, :mid]
        for way in (0, 1):
            start(opp_copies[way][i])
    terms = [share(1, 1), share(3, 1)]
    for i, rows in enumerate(pieces):
        for way in (0, 1):
            piece = terms[way][i * group : (i + 1) * group]
            opp_copies[way][i].wait_recv()
            arrived = opp_in[way, rows, :].astype(F32)
            low, high = piece[:, :mid], piece[:, mid:]
            if way == 0:
                high = high + arrived
            else:
                low = low + arrived
            full_out[way, 1, rows, :mid] = low.astype(BF)
            full_out[way, 1, rows, mid:] = high.astype(BF)
            start(full_copies[way][1][i])
    term = share(0, 0)
    for i, rows in enumerate(pieces):
        piece = term[i * group : (i + 1) * group]
        for way in (0, 1):
            full_copies[way][0][i].wait_recv()
            piece = piece + full_in[way, 0, rows, :].astype(F32)
        row_out[rows, :] = piece.astype(BF)
        start(row_copies[i])
    term = share(0, 1)
    for i, rows in enumerate(pieces):
        row_copies[i].wait_recv()
        piece = term[i * group : (i + 1) * group] + row_in[rows, :].astype(F32)
        for way in (0, 1):
            full_copies[way][1][i].wait_recv()
            piece = piece + full_in[way, 1, rows, :].astype(F32)
        gin_ref[rows, :] = piece.astype(BF)

    for copy in sent:
        copy.wait_send()


def hand_on(a_ref, b_ref, a_out, b_out, a_held, b_held, sems):
    arrive = [pltpu.make_async_copy(a_ref, a_held, sems.at[0]), pltpu.make_async_copy(b_ref, b_held, sems.at[1])]
    leave = [pltpu.make_async_copy(a_held, a_out, sems.at[2]), pltpu.make_async_copy(b_held, b_out, sems.at[3])]
    for copy in arrive:
        copy.start()
    for copy, following in zip(arrive, leave):
        copy.wait()
        following.start()
    for copy in leave:
        copy.wait()


def on_device(activations, qkv_weight, grad_out):
    length, depth = activations.shape
    width = grad_out.shape[1]
    half = length // 2
    steps = lax.axis_size("seq") // 8
    weights = jnp.transpose(qkv_weight, (1, 0, 2))
    anywhere = pl.BlockSpec(memory_space=pl.ANY)
    vmem = pl.BlockSpec(memory_space=pltpu.VMEM)
    dma = pltpu.SemaphoreType.DMA
    attention, grad_input = pl.pallas_call(
        kernel,
        out_shape=(
            jax.ShapeDtypeStruct((length, width), BF),
            jax.ShapeDtypeStruct((half, depth), BF),
        ),
        in_specs=[anywhere] * 3,
        out_specs=(vmem, vmem),
        scratch_shapes=[
            pltpu.VMEM((4, length, depth), BF),
            pltpu.VMEM((4, depth, 3 * width), BF),
            pltpu.VMEM((length, 3 * width), F32),
            pltpu.VMEM((HEADS, length, HEAD), BF),
            pltpu.VMEM((HEADS, HEAD, length), BF),
            pltpu.VMEM((HEADS, length, HEAD), BF),
            pltpu.VMEM((HEADS, 2, length, HEAD), BF),
            pltpu.VMEM((HEADS, 2, HEAD, length), BF),
            pltpu.VMEM((HEADS, 2, length, HEAD), BF),
            pltpu.VMEM((HEADS, 2, HEAD, length), BF),
            *[pltpu.VMEM((HEADS, *tile), kind) for kind in (F32, F32, BF, BF) for tile in TILES],
            pltpu.VMEM((length, length), BF),
            pltpu.VMEM((HEADS, length, length), BF),
            pltpu.VMEM((HEADS, 2, length, HEAD), F32),
            pltpu.VMEM((HEADS, 2, length, HEAD), BF),
            pltpu.VMEM((HEADS, 2, length, HEAD), BF),
            pltpu.VMEM((length, 3 * width), BF),
            pltpu.VMEM((half, depth), BF),
            pltpu.VMEM((half, depth), BF),
            pltpu.VMEM((2, half, depth // 2), BF),
            pltpu.VMEM((2, half, depth // 2), BF),
            pltpu.VMEM((2, 2, half, depth), BF),
            pltpu.VMEM((2, 2, half, depth), BF),
            pltpu.VMEM((half, depth), BF),
            pltpu.VMEM((half, depth), BF),
            dma((7,)),
            *[dma((7,))] * 2,
            *[dma((2, 3))] * 2,
            *[dma((2,))] * 4,
            *[dma((2, steps, 2))] * 2,
            *[dma((2 * steps,))] * 2,
            *[dma((2, 2 * steps))] * 2,
            *[dma((HEADS + 1,))] * 2,
            *[dma((HEADS - 1 + GROUPS,))] * 2,
            *[dma((GROUPS // 2,))] * 2,
            *[dma((2, GROUPS // 2))] * 2,
            *[dma((2, 2, GROUPS // 2))] * 2,
            *[dma((GROUPS // 2,))] * 2,
        ],
        compiler_params=pltpu.CompilerParams(
            collective_id=0, has_side_effects=True, vmem_limit_bytes=60 * 2**20
        ),
    )(activations, weights, grad_out)
    return pl.pallas_call(
        hand_on,
        out_shape=(
            jax.ShapeDtypeStruct((length, width), BF),
            jax.ShapeDtypeStruct((half, depth), BF),
        ),
        in_specs=[anywhere] * 2,
        out_specs=(anywhere, anywhere),
        scratch_shapes=[pltpu.VMEM((length, width), BF), pltpu.VMEM((half, depth), BF), dma((4,))],
        compiler_params=pltpu.CompilerParams(vmem_limit_bytes=60 * 2**20),
    )(attention, grad_input)


def solution(mesh):
    in_specs = (P("seq", "col"), P("col", None, "row"), P("seq", ("row", "col")))
    out_specs = (P("seq", ("row", "col")), P(("seq", "row"), "col"))
    return jax.shard_map(on_device, mesh=mesh, in_specs=in_specs, out_specs=out_specs, check_vma=False)
```

```python
import functools

import jax
import jax.numpy as jnp
from jax import lax
from jax.experimental import pallas as pl
from jax.experimental.pallas import tpu as pltpu
from jax.sharding import PartitionSpec as P

HEAD = 128
HEADS = 3
GROUPS = 4
TILES = ((256, 256), (512, 256), (640, 128))
LOG2E = 1.4426950408889634
MESH = pl.DeviceIdType.MESH
BF = jnp.bfloat16
F32 = jnp.float32
PLACE = (2, 0, 1)


def dot(a, b):
    return jnp.dot(a, b, preferred_element_type=F32)


def dot_nt(a, b):
    return lax.dot_general(a, b, (((1,), (1,)), ((), ())), preferred_element_type=F32)


def kernel(
    act_hbm, w_hbm, go_hbm, attn_ref, gin_ref,
    act, w, acc, go, go_t, query, pair, pair_t, prior, prior_t,
    stats, e_a, e_b, e_c, dp_a, dp_b, dp_c, p_a, p_b, p_c, ds_a, ds_b, ds_c, p_prior, ds_prior,
    own_grad, sent_grad, back_grad, grads, cross_out, cross_in, opp_out, opp_in, full_out, full_in, row_out, row_in,
    local_sem, inj_send, inj_recv, act_send, act_recv, fwd_send, fwd_recv, swap_send, swap_recv,
    z_send, z_recv, y_send, y_recv, core_send, core_recv, kv_send, kv_recv, gr_send, gr_recv,
    cross_send, cross_recv, opp_send, opp_recv, full_send, full_recv, row_send, row_recv,
):
    seq, row, col = lax.axis_index("seq"), lax.axis_index("row"), lax.axis_index("col")
    n_seq = lax.axis_size("seq")
    n_z = n_seq // 4
    z, side, core = seq // 4, (seq // 2) % 2, seq % 2
    length, depth = act_hbm.shape
    width = go_hbm.shape[1]
    total = 3 * width
    half = length // 2
    group = length // GROUPS
    part = depth // (2 * n_z)

    def at_col(step):
        return (seq, row, (col + step) % 4)

    def at_seq(index):
        return (index, row, col)

    right, opposite, left = at_col(1), at_col(2), at_col(3)
    up, down = at_seq((seq + 4) % n_seq), at_seq((seq + n_seq - 4) % n_seq)
    twin = at_seq(seq + 1 - 2 * core)
    beside = at_seq(seq + 2 - 4 * side)
    following, previous = at_seq((seq + 1) % n_seq), at_seq((seq + n_seq - 1) % n_seq)
    partner = (seq, 1 - row, col)
    sent = []

    def remote(src, dst, send, recv, device):
        return pltpu.make_async_remote_copy(
            src_ref=src, dst_ref=dst, send_sem=send, recv_sem=recv, device_id=device, device_id_type=MESH
        )

    def start(copy):
        copy.start()
        sent.append(copy)

    own_cols = pl.ds(pl.multiple_of(col * width, 128), width)
    locals_ = [pltpu.make_async_copy(act_hbm, act.at[0], local_sem.at[0])]
    for kind in range(3):
        at = PLACE[kind] * width
        locals_.append(
            pltpu.make_async_copy(w_hbm.at[kind, :, own_cols], w.at[0, :, at : at + width], local_sem.at[1 + kind])
        )
    for head in range(HEADS):
        locals_.append(
            pltpu.make_async_copy(
                go_hbm.at[:, head * HEAD : (head + 1) * HEAD], go.at[head], local_sem.at[4 + head]
            )
        )
    for copy in locals_:
        copy.start()

    barrier = pltpu.get_barrier_semaphore()
    friends = (right, opposite, left, up, down, twin, beside, following, previous, partner)
    for friend in friends:
        pl.semaphore_signal(barrier, inc=1, device_id=friend, device_id_type=MESH)
    pl.semaphore_wait(barrier, len(friends))

    def rows_of(z_at, core_at):
        return pl.ds(pl.multiple_of(z_at * (2 * part) + core_at * part, 16), part)

    mine = rows_of(z, core)
    only = 1 + 2 * side

    def inject(index, kind, step):
        cols = pl.ds(pl.multiple_of(((col + step) % 4) * width, 128), width)
        at = PLACE[kind] * width
        return remote(
            w_hbm.at[kind, mine, cols], w.at[4 - step, mine, at : at + width],
            inj_send.at[index], inj_recv.at[index], at_col(step),
        )

    pair_injections = [
        inject(index, kind, step)
        for index, (kind, step) in enumerate(((1, 2), (2, 2), (1, 1), (2, 1), (1, 3), (2, 3)))
    ]
    query_injections = [inject(6 + index, 0, step) for index, step in enumerate((2, 1, 3))]

    early_at, late_at = row * half, (1 - row) * half
    early, late = (pl.ds(pl.multiple_of(at, 64), half) for at in (early_at, late_at))
    quarters = [pl.ds(pl.multiple_of(early_at + i * group, 32), group) for i in (0, 1)]

    def own_act(index, way):
        rows = (quarters[way], quarters[1 - way], late)[index]
        return remote(
            act_hbm.at[rows], act.at[3 - 2 * way, rows], act_send.at[way, index], act_recv.at[way, index],
            (right, left)[way],
        )

    def far_act(way):
        rows = quarters[way]
        there = act.at[2, rows]
        return (
            remote(act.at[3 - 2 * way, rows], there, fwd_send.at[way], fwd_recv.at[way], (right, left)[way]),
            remote(there, there, swap_send.at[way], swap_recv.at[way], partner),
        )

    own_acts = [[own_act(index, way) for way in (0, 1)] for index in range(3)]
    far_acts = [far_act(way) for way in (0, 1)]
    for copy in pair_injections + own_acts[0] + query_injections:
        start(copy)

    def pass_on():
        for way in (0, 1):
            own_acts[0][way].wait_recv()
            start(far_acts[way][0])
        for copies in own_acts[1:]:
            for copy in copies:
                start(copy)

    def hand_over():
        for copy, swap in far_acts:
            copy.wait_recv()
            start(swap)

    for copy in locals_[:4]:
        copy.wait()

    @pl.loop(0, 2)
    def _(i):
        rows = pl.ds(pl.multiple_of(i * half, half), half)
        acc[rows, :] = dot(act[0, rows, :], w[0])

    for copy in locals_[4:]:
        copy.wait()
    for head in range(HEADS):
        go_t[head] = jnp.transpose(go[head])

    def ring(way, step):
        origin = (z + n_z - step) % n_z if way == 0 else (z + step) % n_z
        rows = rows_of(origin, core)
        if step < n_z // 2 - 1:
            blocks = [w.at[1:4, rows, 0 : 2 * width], w.at[1:4, rows, 2 * width : total]]
        elif way == 0:
            blocks = [w.at[1:4, rows, 0:width], w.at[1:3, rows, 2 * width : total]]
        else:
            blocks = [w.at[1:4, rows, width : 2 * width], w.at[3, rows, 2 * width : total]]
        return [
            remote(block, block, z_send.at[way, step, i], z_recv.at[way, step, i], (up, down)[way])
            for i, block in enumerate(blocks)
        ]

    steps = n_z // 2
    origins = [[z]]
    for step in range(1, steps):
        origins.append([(z + n_z - step) % n_z, (z + step) % n_z])
    origins.append([(z + steps) % n_z])

    def spread(index, origin):
        rows = rows_of(origin, core)
        blocks = (w.at[only, rows, 0 : 2 * width], w.at[1:4, rows, 0 : 2 * width], w.at[1:4, rows, 2 * width : total])
        return (
            remote(blocks[0], blocks[0], y_send.at[index], y_recv.at[index], beside),
            remote(blocks[1], blocks[1], core_send.at[0, index], core_recv.at[0, index], twin),
            remote(blocks[2], blocks[2], core_send.at[1, index], core_recv.at[1, index], twin),
        )

    rings = [[ring(way, step) for way in (0, 1)] for step in range(steps)]
    spreads, count = [], 0
    for members in origins:
        spreads.append([spread(count + i, origin) for i, origin in enumerate(members)])
        count += len(members)

    def across_pairs(step):
        for exchange, across, _ in spreads[step]:
            start(across)

    def turn_pairs(step):
        for way in (0, 1):
            if step > 0:
                rings[step - 1][way][0].wait_recv()
            if step < steps:
                start(rings[step][way][0])
        if step > 0:
            across_pairs(step - 1)

    def turn_queries(step):
        for way in (0, 1):
            if step > 0:
                rings[step - 1][way][1].wait_recv()
            if step < steps:
                start(rings[step][way][1])
        for _, _, across in spreads[step]:
            start(across)

    for copy in pair_injections:
        copy.wait_recv()
    turn_pairs(0)
    turn_pairs(1)
    for copy in query_injections:
        copy.wait_recv()
    turn_queries(0)
    pass_on()
    turn_pairs(2)
    turn_queries(1)
    hand_over()
    turn_pairs(3)
    turn_queries(2)
    turn_pairs(4)
    across_pairs(steps)
    turn_queries(3)
    for members in spreads:
        for _, across, _ in members:
            across.wait_recv()

    def keep_pairs(rows, done):
        for head in range(HEADS):
            for kind in range(2):
                at = kind * width + head * HEAD
                pair[head, kind, rows, :] = done[:, at : at + HEAD].astype(BF)

    def keep_queries(rows, done):
        for head in range(HEADS):
            query[head, rows, :] = done[:, head * HEAD : (head + 1) * HEAD].astype(BF)

    def kv_copy(index, heads, rows):
        return remote(
            pair.at[heads, :, rows, :], prior.at[heads, :, rows, :], kv_send.at[index], kv_recv.at[index], following
        )

    kv_copies = [kv_copy(HEADS, pl.ds(0, HEADS), early)]
    kv_copies += [kv_copy(head, pl.ds(head, 1), late) for head in range(HEADS)]
    for copy in own_acts[1]:
        copy.wait_recv()

    def product(rows, cols):
        return acc[rows, cols] + sum(dot(act[index, rows, :], w[index, :, cols]) for index in (1, 2, 3))

    pair_cols, query_cols = pl.ds(0, 2 * width), pl.ds(2 * width, width)
    keep_pairs(early, product(early, pair_cols))
    start(kv_copies[0])
    for copy in own_acts[2]:
        copy.wait_recv()
    for _, swap in far_acts:
        swap.wait_recv()
    keep_pairs(late, product(late, pair_cols))
    for copy in kv_copies[1:]:
        start(copy)
    turn_queries(4)
    for members in spreads:
        for _, _, across in members:
            across.wait_recv()
    for rows in (early, late):
        keep_queries(rows, product(rows, query_cols))
    for head in range(HEADS):
        for kind in range(2):
            pair_t[head, kind] = jnp.transpose(pair[head, kind])

    scaling = HEAD**-0.5
    base = scaling * LOG2E
    has_prior = seq > 0
    tiles = (
        (0, 256, e_a, dp_a, p_a, ds_a),
        (256, 256, e_b, dp_b, p_b, ds_b),
        (512, 128, e_c, dp_c, p_c, ds_c),
    )
    for head in range(HEADS):
        for q0, size, e_own, dp_own, _, _ in tiles:
            seen = q0 + size
            scores = dot_nt(pair[head, 0, 0:seen, :], query[head, q0:seen, :])
            key_at = lax.broadcasted_iota(jnp.int32, (seen, size), 0)
            query_at = lax.broadcasted_iota(jnp.int32, (seen, size), 1) + q0
            scores = jnp.where(key_at <= query_at, scores, -jnp.inf) * base
            highest = jnp.max(scores, axis=0, keepdims=True)
            raised = jnp.exp2(scores - highest)
            e_own[head] = raised
            stats[head, 0:1, q0:seen] = highest
            stats[head, 1:2, q0:seen] = jnp.sum(raised, axis=0, keepdims=True)
            dp_own[head] = dot_nt(pair[head, 1, 0:seen, :], go[head, q0:seen, :])

    order = [
        pl.ds(pl.multiple_of(at * half + i * group, 32), group) for at in (1 - row, row) for i in range(GROUPS // 2)
    ]
    gr_copies = [
        remote(sent_grad.at[head], back_grad.at[head], gr_send.at[head], gr_recv.at[head], previous)
        for head in range(HEADS - 1)
    ]
    gr_copies += [
        remote(
            sent_grad.at[HEADS - 1, :, rows, :], back_grad.at[HEADS - 1, :, rows, :],
            gr_send.at[HEADS - 1 + i], gr_recv.at[HEADS - 1 + i], previous,
        )
        for i, rows in enumerate(order)
    ]
    for head in range(HEADS):
        if head == 0:
            kv_copies[0].wait_recv()
        kv_copies[1 + head].wait_recv()
        for kind in range(2):
            prior_t[head, kind] = jnp.transpose(prior[head, kind])
        for q0, size, e_own, dp_own, p_own, ds_own in tiles:
            seen = q0 + size
            s_prior = dot_nt(prior[head, 0], query[head, q0:seen, :])
            own_top, own_sum = stats[head, 0:1, q0:seen], stats[head, 1:2, q0:seen]
            prior_top = jnp.where(has_prior, jnp.max(s_prior, axis=0, keepdims=True) * base, -jnp.inf)
            highest = jnp.maximum(own_top, prior_top)
            e_prior = jnp.exp2(s_prior * base - jnp.where(has_prior, highest, jnp.inf))
            shrink = jnp.exp2(own_top - highest)
            inverse = 1.0 / (own_sum * shrink + jnp.sum(e_prior, axis=0, keepdims=True))
            w_own, w_prior = e_own[head] * (shrink * inverse), e_prior * inverse
            b_own, b_prior = w_own.astype(BF), w_prior.astype(BF)
            p_own[head] = b_own
            p_prior[:, q0:seen] = b_prior
            ctx_t = dot(prior_t[head, 1], b_prior) + dot(pair_t[head, 1, :, 0:seen], b_own)
            delta = jnp.sum(go_t[head, :, q0:seen].astype(F32) * ctx_t, axis=0, keepdims=True)
            attn_ref[q0:seen, head * HEAD : (head + 1) * HEAD] = jnp.transpose(ctx_t).astype(BF)
            ds_own[head] = (w_own * (dp_own[head] - delta)).astype(BF)
            dp_prior = dot_nt(prior[head, 1], go[head, q0:seen, :])
            ds_prior[head, :, q0:seen] = (w_prior * (dp_prior - delta)).astype(BF)
        if head < HEADS - 1:
            sent_grad[head, 0] = (dot(ds_prior[head], query[head]) * scaling).astype(BF)
            sent_grad[head, 1] = dot(p_prior[...], go[head]).astype(BF)
            start(gr_copies[head])
        else:
            for i, rows in enumerate(order):
                sent_grad[head, 0, rows, :] = (dot(ds_prior[head, rows, :], query[head]) * scaling).astype(BF)
                sent_grad[head, 1, rows, :] = dot(p_prior[rows, :], go[head]).astype(BF)
                start(gr_copies[head + i])

    for head in range(HEADS):
        for q0, size, _, _, p_own, ds_own in tiles:
            seen = q0 + size
            dq_t = dot(prior_t[head, 0], ds_prior[head, :, q0:seen]) + dot(pair_t[head, 0, :, 0:seen], ds_own[head])
            at = 2 * width + head * HEAD
            grads[q0:seen, at : at + HEAD] = (jnp.transpose(dq_t) * scaling).astype(BF)
            terms = (dot(ds_own[head], query[head, q0:seen, :]) * scaling, dot(p_own[head], go[head, q0:seen, :]))
            for kind in range(2):
                if q0:
                    own_grad[head, kind, 0:q0, :] = own_grad[head, kind, 0:q0, :] + terms[kind][0:q0]
                own_grad[head, kind, q0:seen, :] = terms[kind][q0:seen]

    mid = depth // 2
    halves = [pl.ds(pl.multiple_of(at * half, half), half) for at in (1 - row, row)]
    pieces = [pl.ds(i * group, group) for i in range(GROUPS // 2)]

    def collect(which):
        if which == 0:
            for head in range(HEADS - 1):
                gr_copies[head].wait_recv()
        for i in range(GROUPS // 2):
            gr_copies[HEADS - 1 + which * (GROUPS // 2) + i].wait_recv()
        rows = halves[which]
        for head in range(HEADS):
            for kind in range(2):
                at = kind * width + head * HEAD
                back = back_grad[head, kind, rows, :].astype(F32)
                grads[rows, at : at + HEAD] = (own_grad[head, kind, rows, :] + back).astype(BF)

    def share(index, which):
        return dot_nt(grads[halves[which], :], w[index])

    cross_copies = [
        remote(cross_out.at[rows], cross_in.at[rows], cross_send.at[i], cross_recv.at[i], partner)
        for i, rows in enumerate(pieces)
    ]
    row_copies = [
        remote(row_out.at[rows], row_in.at[rows], row_send.at[i], row_recv.at[i], partner)
        for i, rows in enumerate(pieces)
    ]
    opp_copies = [
        [
            remote(opp_out.at[way, rows], opp_in.at[way, rows], opp_send.at[way, i], opp_recv.at[way, i], (right, left)[way])
            for i, rows in enumerate(pieces)
        ]
        for way in (0, 1)
    ]
    full_copies = [
        [
            [
                remote(
                    full_out.at[way, which, rows], full_in.at[way, which, rows],
                    full_send.at[way, which, i], full_recv.at[way, which, i], (right, left)[way],
                )
                for i, rows in enumerate(pieces)
            ]
            for which in (0, 1)
        ]
        for way in (0, 1)
    ]

    collect(0)
    for way in (0, 1):
        full_out[way, 0] = share((1, 3)[way], 0).astype(BF)
        for copy in full_copies[way][0]:
            start(copy)
    cross_out[...] = share(2, 0).astype(BF)
    for copy in cross_copies:
        start(copy)
    collect(1)
    term = share(2, 1)
    for i, rows in enumerate(pieces):
        cross_copies[i].wait_recv()
        summed = (term[i * group : (i + 1) * group] + cross_in[rows, :].astype(F32)).astype(BF)
        opp_out[0, rows, :] = summed[:, mid:]
        opp_out[1, rows, :] = summed[:, :mid]
        for way in (0, 1):
            start(opp_copies[way][i])
    terms = [share(1, 1), share(3, 1)]
    for i, rows in enumerate(pieces):
        for way in (0, 1):
            piece = terms[way][i * group : (i + 1) * group]
            opp_copies[way][i].wait_recv()
            arrived = opp_in[way, rows, :].astype(F32)
            low, high = piece[:, :mid], piece[:, mid:]
            if way == 0:
                high = high + arrived
            else:
                low = low + arrived
            full_out[way, 1, rows, :mid] = low.astype(BF)
            full_out[way, 1, rows, mid:] = high.astype(BF)
            start(full_copies[way][1][i])
    term = share(0, 0)
    for i, rows in enumerate(pieces):
        piece = term[i * group : (i + 1) * group]
        for way in (0, 1):
            full_copies[way][0][i].wait_recv()
            piece = piece + full_in[way, 0, rows, :].astype(F32)
        row_out[rows, :] = piece.astype(BF)
        start(row_copies[i])
    term = share(0, 1)
    for i, rows in enumerate(pieces):
        row_copies[i].wait_recv()
        piece = term[i * group : (i + 1) * group] + row_in[rows, :].astype(F32)
        for way in (0, 1):
            full_copies[way][1][i].wait_recv()
            piece = piece + full_in[way, 1, rows, :].astype(F32)
        gin_ref[rows, :] = piece.astype(BF)

    for copy in sent:
        copy.wait_send()


def hand_on(a_ref, b_ref, a_out, b_out, a_held, b_held, sems):
    arrive = [pltpu.make_async_copy(a_ref, a_held, sems.at[0]), pltpu.make_async_copy(b_ref, b_held, sems.at[1])]
    leave = [pltpu.make_async_copy(a_held, a_out, sems.at[2]), pltpu.make_async_copy(b_held, b_out, sems.at[3])]
    for copy in arrive:
        copy.start()
    for copy, following in zip(arrive, leave):
        copy.wait()
        following.start()
    for copy in leave:
        copy.wait()


def on_device(activations, qkv_weight, grad_out):
    length, depth = activations.shape
    width = grad_out.shape[1]
    half = length // 2
    steps = lax.axis_size("seq") // 8
    weights = jnp.transpose(qkv_weight, (1, 0, 2))
    anywhere = pl.BlockSpec(memory_space=pl.ANY)
    vmem = pl.BlockSpec(memory_space=pltpu.VMEM)
    dma = pltpu.SemaphoreType.DMA
    attention, grad_input = pl.pallas_call(
        kernel,
        out_shape=(
            jax.ShapeDtypeStruct((length, width), BF),
            jax.ShapeDtypeStruct((half, depth), BF),
        ),
        in_specs=[anywhere] * 3,
        out_specs=(vmem, vmem),
        scratch_shapes=[
            pltpu.VMEM((4, length, depth), BF),
            pltpu.VMEM((4, depth, 3 * width), BF),
            pltpu.VMEM((length, 3 * width), F32),
            pltpu.VMEM((HEADS, length, HEAD), BF),
            pltpu.VMEM((HEADS, HEAD, length), BF),
            pltpu.VMEM((HEADS, length, HEAD), BF),
            pltpu.VMEM((HEADS, 2, length, HEAD), BF),
            pltpu.VMEM((HEADS, 2, HEAD, length), BF),
            pltpu.VMEM((HEADS, 2, length, HEAD), BF),
            pltpu.VMEM((HEADS, 2, HEAD, length), BF),
            pltpu.VMEM((HEADS, 2, length), F32),
            *[pltpu.VMEM((HEADS, *tile), kind) for kind in (F32, F32, BF, BF) for tile in TILES],
            pltpu.VMEM((length, length), BF),
            pltpu.VMEM((HEADS, length, length), BF),
            pltpu.VMEM((HEADS, 2, length, HEAD), F32),
            pltpu.VMEM((HEADS, 2, length, HEAD), BF),
            pltpu.VMEM((HEADS, 2, length, HEAD), BF),
            pltpu.VMEM((length, 3 * width), BF),
            pltpu.VMEM((half, depth), BF),
            pltpu.VMEM((half, depth), BF),
            pltpu.VMEM((2, half, depth // 2), BF),
            pltpu.VMEM((2, half, depth // 2), BF),
            pltpu.VMEM((2, 2, half, depth), BF),
            pltpu.VMEM((2, 2, half, depth), BF),
            pltpu.VMEM((half, depth), BF),
            pltpu.VMEM((half, depth), BF),
            dma((7,)),
            *[dma((9,))] * 2,
            *[dma((2, 3))] * 2,
            *[dma((2,))] * 4,
            *[dma((2, steps, 2))] * 2,
            *[dma((2 * steps,))] * 2,
            *[dma((2, 2 * steps))] * 2,
            *[dma((HEADS + 1,))] * 2,
            *[dma((HEADS - 1 + GROUPS,))] * 2,
            *[dma((GROUPS // 2,))] * 2,
            *[dma((2, GROUPS // 2))] * 2,
            *[dma((2, 2, GROUPS // 2))] * 2,
            *[dma((GROUPS // 2,))] * 2,
        ],
        compiler_params=pltpu.CompilerParams(
            collective_id=0, has_side_effects=True, vmem_limit_bytes=60 * 2**20
        ),
    )(activations, weights, grad_out)
    return pl.pallas_call(
        hand_on,
        out_shape=(
            jax.ShapeDtypeStruct((length, width), BF),
            jax.ShapeDtypeStruct((half, depth), BF),
        ),
        in_specs=[anywhere] * 2,
        out_specs=(anywhere, anywhere),
        scratch_shapes=[pltpu.VMEM((length, width), BF), pltpu.VMEM((half, depth), BF), dma((4,))],
        compiler_params=pltpu.CompilerParams(vmem_limit_bytes=60 * 2**20),
    )(attention, grad_input)


def solution(mesh):
    in_specs = (P("seq", "col"), P("col", None, "row"), P("seq", ("row", "col")))
    out_specs = (P("seq", ("row", "col")), P(("seq", "row"), "col"))
    return jax.shard_map(on_device, mesh=mesh, in_specs=in_specs, out_specs=out_specs, check_vma=False)
```

```python
import functools

import jax
import jax.numpy as jnp
from jax import lax
from jax.experimental import pallas as pl
from jax.experimental.pallas import tpu as pltpu
from jax.sharding import PartitionSpec as P

HEAD = 128
HEADS = 3
GROUPS = 4
TILES = ((256, 256), (512, 256), (640, 128))
LOG2E = 1.4426950408889634
MESH = pl.DeviceIdType.MESH
BF = jnp.bfloat16
F32 = jnp.float32
PLACE = (2, 0, 1)


def dot(a, b):
    return jnp.dot(a, b, preferred_element_type=F32)


def dot_nt(a, b):
    return lax.dot_general(a, b, (((1,), (1,)), ((), ())), preferred_element_type=F32)


def kernel(
    act_hbm, w_hbm, go_hbm, attn_ref, gin_ref,
    act, w, acc, go, go_t, query, pair, pair_t, prior, prior_t,
    stats, e_a, e_b, e_c, dp_a, dp_b, dp_c, p_a, p_b, p_c, ds_a, ds_b, ds_c, p_prior, ds_prior,
    own_grad, sent_grad, back_grad, grads, cross_out, cross_in, opp_out, opp_in, full_out, full_in, row_out, row_in,
    local_sem, inj_send, inj_recv, act_send, act_recv, fwd_send, fwd_recv, swap_send, swap_recv,
    z_send, z_recv, core_send, core_recv, kv_send, kv_recv, gr_send, gr_recv,
    cross_send, cross_recv, opp_send, opp_recv, full_send, full_recv, row_send, row_recv,
):
    seq, row, col = lax.axis_index("seq"), lax.axis_index("row"), lax.axis_index("col")
    n_seq = lax.axis_size("seq")
    n_z = n_seq // 4
    z, core = seq // 4, seq % 2
    length, depth = act_hbm.shape
    width = go_hbm.shape[1]
    total = 3 * width
    half = length // 2
    group = length // GROUPS
    part = depth // (2 * n_z)

    def at_col(step):
        return (seq, row, (col + step) % 4)

    def at_seq(index):
        return (index, row, col)

    right, opposite, left = at_col(1), at_col(2), at_col(3)
    up, down = at_seq((seq + 4) % n_seq), at_seq((seq + n_seq - 4) % n_seq)
    twin = at_seq(seq + 1 - 2 * core)
    following, previous = at_seq((seq + 1) % n_seq), at_seq((seq + n_seq - 1) % n_seq)
    partner = (seq, 1 - row, col)
    sent = []

    def remote(src, dst, send, recv, device):
        return pltpu.make_async_remote_copy(
            src_ref=src, dst_ref=dst, send_sem=send, recv_sem=recv, device_id=device, device_id_type=MESH
        )

    def start(copy):
        copy.start()
        sent.append(copy)

    own_cols = pl.ds(pl.multiple_of(col * width, 128), width)
    locals_ = [pltpu.make_async_copy(act_hbm, act.at[0], local_sem.at[0])]
    for kind in range(3):
        at = PLACE[kind] * width
        locals_.append(
            pltpu.make_async_copy(w_hbm.at[kind, :, own_cols], w.at[0, :, at : at + width], local_sem.at[1 + kind])
        )
    for head in range(HEADS):
        locals_.append(
            pltpu.make_async_copy(
                go_hbm.at[:, head * HEAD : (head + 1) * HEAD], go.at[head], local_sem.at[4 + head]
            )
        )
    for copy in locals_:
        copy.start()

    barrier = pltpu.get_barrier_semaphore()
    friends = (right, opposite, left, up, down, twin, following, previous, partner)
    for friend in friends:
        pl.semaphore_signal(barrier, inc=1, device_id=friend, device_id_type=MESH)
    pl.semaphore_wait(barrier, len(friends))

    def rows_of(z_at, core_at):
        return pl.ds(pl.multiple_of(z_at * (2 * part) + core_at * part, 16), part)

    mine = rows_of(z, core)

    def inject(index, kind, step, rows):
        cols = pl.ds(pl.multiple_of(((col + step) % 4) * width, 128), width)
        at = PLACE[kind] * width
        return remote(
            w_hbm.at[kind, rows, cols], w.at[4 - step, rows, at : at + width],
            inj_send.at[index], inj_recv.at[index], at_col(step),
        )

    kinds_steps = ((1, 2), (2, 2), (1, 1), (2, 1), (1, 3), (2, 3))
    across_z = rows_of((z + n_z // 2) % n_z, core)
    pair_injections = [inject(index, *member, mine) for index, member in enumerate(kinds_steps)]
    far_injections = [inject(6 + index, *member, across_z) for index, member in enumerate(kinds_steps)]
    query_injections = [inject(12 + index, 0, step, mine) for index, step in enumerate((2, 1, 3))]

    early_at, late_at = row * half, (1 - row) * half
    early, late = (pl.ds(pl.multiple_of(at, 64), half) for at in (early_at, late_at))
    quarters = [pl.ds(pl.multiple_of(early_at + i * group, 32), group) for i in (0, 1)]

    def own_act(index, way):
        rows = (quarters[way], quarters[1 - way], late)[index]
        return remote(
            act_hbm.at[rows], act.at[3 - 2 * way, rows], act_send.at[way, index], act_recv.at[way, index],
            (right, left)[way],
        )

    def far_act(way):
        rows = quarters[way]
        there = act.at[2, rows]
        return (
            remote(act.at[3 - 2 * way, rows], there, fwd_send.at[way], fwd_recv.at[way], (right, left)[way]),
            remote(there, there, swap_send.at[way], swap_recv.at[way], partner),
        )

    own_acts = [[own_act(index, way) for way in (0, 1)] for index in range(3)]
    far_acts = [far_act(way) for way in (0, 1)]
    for copy in pair_injections + own_acts[0] + query_injections:
        start(copy)

    def pass_on():
        for way in (0, 1):
            own_acts[0][way].wait_recv()
            start(far_acts[way][0])
        for copy in own_acts[1] + far_injections + own_acts[2]:
            start(copy)

    def hand_over():
        for copy, swap in far_acts:
            copy.wait_recv()
            start(swap)

    for copy in locals_[:4]:
        copy.wait()

    @pl.loop(0, 2)
    def _(i):
        rows = pl.ds(pl.multiple_of(i * half, half), half)
        acc[rows, :] = dot(act[0, rows, :], w[0])

    for copy in locals_[4:]:
        copy.wait()
    for head in range(HEADS):
        go_t[head] = jnp.transpose(go[head])

    def ring(way, step):
        origin = (z + n_z - step) % n_z if way == 0 else (z + step) % n_z
        rows = rows_of(origin, core)
        if step < n_z // 2 - 1:
            blocks = [w.at[1:4, rows, 0 : 2 * width], w.at[1:4, rows, 2 * width : total]]
        else:
            blocks = [None, w.at[1:3, rows, 2 * width : total] if way == 0 else w.at[3, rows, 2 * width : total]]
        return [
            remote(block, block, z_send.at[way, step, i], z_recv.at[way, step, i], (up, down)[way])
            if block is not None else None
            for i, block in enumerate(blocks)
        ]

    steps = n_z // 2
    origins = [[z]]
    for step in range(1, steps):
        origins.append([(z + n_z - step) % n_z, (z + step) % n_z])
    origins.append([(z + steps) % n_z])

    def spread(index, origin):
        rows = rows_of(origin, core)
        blocks = (w.at[1:4, rows, 0 : 2 * width], w.at[1:4, rows, 2 * width : total])
        return [
            remote(block, block, core_send.at[i, index], core_recv.at[i, index], twin) for i, block in enumerate(blocks)
        ]

    rings = [[ring(way, step) for way in (0, 1)] for step in range(steps)]
    spreads, count = [], 0
    for members in origins:
        spreads.append([spread(count + i, origin) for i, origin in enumerate(members)])
        count += len(members)

    def across_pairs(step):
        for across, _ in spreads[step]:
            start(across)

    def turn_pairs(step):
        for way in (0, 1):
            if step > 0:
                rings[step - 1][way][0].wait_recv()
            if step < steps - 1:
                start(rings[step][way][0])
        if step > 0:
            across_pairs(step - 1)

    def turn_queries(step):
        for way in (0, 1):
            if step > 0:
                rings[step - 1][way][1].wait_recv()
            if step < steps:
                start(rings[step][way][1])
        for _, across in spreads[step]:
            start(across)

    for copy in pair_injections:
        copy.wait_recv()
    turn_pairs(0)
    turn_pairs(1)
    for copy in query_injections:
        copy.wait_recv()
    turn_queries(0)
    pass_on()
    turn_pairs(2)
    turn_queries(1)
    hand_over()
    turn_pairs(3)
    turn_queries(2)
    across_pairs(3)
    for copy in far_injections:
        copy.wait_recv()
    across_pairs(steps)
    turn_queries(3)
    for members in spreads:
        for across, _ in members:
            across.wait_recv()

    def keep_pairs(rows, done):
        for head in range(HEADS):
            for kind in range(2):
                at = kind * width + head * HEAD
                pair[head, kind, rows, :] = done[:, at : at + HEAD].astype(BF)

    def keep_queries(rows, done):
        for head in range(HEADS):
            query[head, rows, :] = done[:, head * HEAD : (head + 1) * HEAD].astype(BF)

    def kv_copy(index, heads, rows):
        return remote(
            pair.at[heads, :, rows, :], prior.at[heads, :, rows, :], kv_send.at[index], kv_recv.at[index], following
        )

    kv_copies = [kv_copy(HEADS, pl.ds(0, HEADS), early)]
    kv_copies += [kv_copy(head, pl.ds(head, 1), late) for head in range(HEADS)]
    for copy in own_acts[1]:
        copy.wait_recv()

    def product(rows, cols):
        return acc[rows, cols] + sum(dot(act[index, rows, :], w[index, :, cols]) for index in (1, 2, 3))

    pair_cols, query_cols = pl.ds(0, 2 * width), pl.ds(2 * width, width)
    keep_pairs(early, product(early, pair_cols))
    start(kv_copies[0])
    for copy in own_acts[2]:
        copy.wait_recv()
    for _, swap in far_acts:
        swap.wait_recv()
    keep_pairs(late, product(late, pair_cols))
    for copy in kv_copies[1:]:
        start(copy)
    turn_queries(4)
    for members in spreads:
        for _, across in members:
            across.wait_recv()
    for rows in (early, late):
        keep_queries(rows, product(rows, query_cols))
    for head in range(HEADS):
        for kind in range(2):
            pair_t[head, kind] = jnp.transpose(pair[head, kind])

    scaling = HEAD**-0.5
    base = scaling * LOG2E
    has_prior = seq > 0
    tiles = (
        (0, 256, e_a, dp_a, p_a, ds_a),
        (256, 256, e_b, dp_b, p_b, ds_b),
        (512, 128, e_c, dp_c, p_c, ds_c),
    )
    for head in range(HEADS):
        for q0, size, e_own, dp_own, _, _ in tiles:
            seen = q0 + size
            scores = dot_nt(pair[head, 0, 0:seen, :], query[head, q0:seen, :])
            key_at = lax.broadcasted_iota(jnp.int32, (seen, size), 0)
            query_at = lax.broadcasted_iota(jnp.int32, (seen, size), 1) + q0
            scores = jnp.where(key_at <= query_at, scores, -jnp.inf) * base
            highest = jnp.max(scores, axis=0, keepdims=True)
            raised = jnp.exp2(scores - highest)
            e_own[head] = raised
            stats[head, 0:1, q0:seen] = highest
            stats[head, 1:2, q0:seen] = jnp.sum(raised, axis=0, keepdims=True)
            dp_own[head] = dot_nt(pair[head, 1, 0:seen, :], go[head, q0:seen, :])

    order = [
        pl.ds(pl.multiple_of(at * half + i * group, 32), group) for at in (1 - row, row) for i in range(GROUPS // 2)
    ]
    gr_copies = [
        remote(sent_grad.at[head], back_grad.at[head], gr_send.at[head], gr_recv.at[head], previous)
        for head in range(HEADS - 1)
    ]
    gr_copies += [
        remote(
            sent_grad.at[HEADS - 1, :, rows, :], back_grad.at[HEADS - 1, :, rows, :],
            gr_send.at[HEADS - 1 + i], gr_recv.at[HEADS - 1 + i], previous,
        )
        for i, rows in enumerate(order)
    ]
    for head in range(HEADS):
        if head == 0:
            kv_copies[0].wait_recv()
        kv_copies[1 + head].wait_recv()
        for kind in range(2):
            prior_t[head, kind] = jnp.transpose(prior[head, kind])
        for q0, size, e_own, dp_own, p_own, ds_own in tiles:
            seen = q0 + size
            s_prior = dot_nt(prior[head, 0], query[head, q0:seen, :])
            own_top, own_sum = stats[head, 0:1, q0:seen], stats[head, 1:2, q0:seen]
            prior_top = jnp.where(has_prior, jnp.max(s_prior, axis=0, keepdims=True) * base, -jnp.inf)
            highest = jnp.maximum(own_top, prior_top)
            e_prior = jnp.exp2(s_prior * base - jnp.where(has_prior, highest, jnp.inf))
            shrink = jnp.exp2(own_top - highest)
            inverse = 1.0 / (own_sum * shrink + jnp.sum(e_prior, axis=0, keepdims=True))
            w_own, w_prior = e_own[head] * (shrink * inverse), e_prior * inverse
            b_own, b_prior = w_own.astype(BF), w_prior.astype(BF)
            p_own[head] = b_own
            p_prior[:, q0:seen] = b_prior
            ctx_t = dot(prior_t[head, 1], b_prior) + dot(pair_t[head, 1, :, 0:seen], b_own)
            delta = jnp.sum(go_t[head, :, q0:seen].astype(F32) * ctx_t, axis=0, keepdims=True)
            attn_ref[q0:seen, head * HEAD : (head + 1) * HEAD] = jnp.transpose(ctx_t).astype(BF)
            ds_own[head] = (w_own * (dp_own[head] - delta)).astype(BF)
            dp_prior = dot_nt(prior[head, 1], go[head, q0:seen, :])
            ds_prior[head, :, q0:seen] = (w_prior * (dp_prior - delta)).astype(BF)
        if head < HEADS - 1:
            sent_grad[head, 0] = (dot(ds_prior[head], query[head]) * scaling).astype(BF)
            sent_grad[head, 1] = dot(p_prior[...], go[head]).astype(BF)
            start(gr_copies[head])
        else:
            for i, rows in enumerate(order):
                sent_grad[head, 0, rows, :] = (dot(ds_prior[head, rows, :], query[head]) * scaling).astype(BF)
                sent_grad[head, 1, rows, :] = dot(p_prior[rows, :], go[head]).astype(BF)
                start(gr_copies[head + i])

    for head in range(HEADS):
        for q0, size, _, _, p_own, ds_own in tiles:
            seen = q0 + size
            dq_t = dot(prior_t[head, 0], ds_prior[head, :, q0:seen]) + dot(pair_t[head, 0, :, 0:seen], ds_own[head])
            at = 2 * width + head * HEAD
            grads[q0:seen, at : at + HEAD] = (jnp.transpose(dq_t) * scaling).astype(BF)
            terms = (dot(ds_own[head], query[head, q0:seen, :]) * scaling, dot(p_own[head], go[head, q0:seen, :]))
            for kind in range(2):
                if q0:
                    own_grad[head, kind, 0:q0, :] = own_grad[head, kind, 0:q0, :] + terms[kind][0:q0]
                own_grad[head, kind, q0:seen, :] = terms[kind][q0:seen]

    mid = depth // 2
    halves = [pl.ds(pl.multiple_of(at * half, half), half) for at in (1 - row, row)]
    pieces = [pl.ds(i * group, group) for i in range(GROUPS // 2)]

    def collect(which):
        if which == 0:
            for head in range(HEADS - 1):
                gr_copies[head].wait_recv()
        for i in range(GROUPS // 2):
            gr_copies[HEADS - 1 + which * (GROUPS // 2) + i].wait_recv()
        rows = halves[which]
        for head in range(HEADS):
            for kind in range(2):
                at = kind * width + head * HEAD
                back = back_grad[head, kind, rows, :].astype(F32)
                grads[rows, at : at + HEAD] = (own_grad[head, kind, rows, :] + back).astype(BF)

    def share(index, which):
        return dot_nt(grads[halves[which], :], w[index])

    cross_copies = [
        remote(cross_out.at[rows], cross_in.at[rows], cross_send.at[i], cross_recv.at[i], partner)
        for i, rows in enumerate(pieces)
    ]
    row_copies = [
        remote(row_out.at[rows], row_in.at[rows], row_send.at[i], row_recv.at[i], partner)
        for i, rows in enumerate(pieces)
    ]
    opp_copies = [
        [
            remote(opp_out.at[way, rows], opp_in.at[way, rows], opp_send.at[way, i], opp_recv.at[way, i], (right, left)[way])
            for i, rows in enumerate(pieces)
        ]
        for way in (0, 1)
    ]
    full_copies = [
        [
            [
                remote(
                    full_out.at[way, which, rows], full_in.at[way, which, rows],
                    full_send.at[way, which, i], full_recv.at[way, which, i], (right, left)[way],
                )
                for i, rows in enumerate(pieces)
            ]
            for which in (0, 1)
        ]
        for way in (0, 1)
    ]

    collect(0)
    for way in (0, 1):
        full_out[way, 0] = share((1, 3)[way], 0).astype(BF)
        for copy in full_copies[way][0]:
            start(copy)
    cross_out[...] = share(2, 0).astype(BF)
    for copy in cross_copies:
        start(copy)
    collect(1)
    term = share(2, 1)
    for i, rows in enumerate(pieces):
        cross_copies[i].wait_recv()
        summed = (term[i * group : (i + 1) * group] + cross_in[rows, :].astype(F32)).astype(BF)
        opp_out[0, rows, :] = summed[:, mid:]
        opp_out[1, rows, :] = summed[:, :mid]
        for way in (0, 1):
            start(opp_copies[way][i])
    terms = [share(1, 1), share(3, 1)]
    for i, rows in enumerate(pieces):
        for way in (0, 1):
            piece = terms[way][i * group : (i + 1) * group]
            opp_copies[way][i].wait_recv()
            arrived = opp_in[way, rows, :].astype(F32)
            low, high = piece[:, :mid], piece[:, mid:]
            if way == 0:
                high = high + arrived
            else:
                low = low + arrived
            full_out[way, 1, rows, :mid] = low.astype(BF)
            full_out[way, 1, rows, mid:] = high.astype(BF)
            start(full_copies[way][1][i])
    term = share(0, 0)
    for i, rows in enumerate(pieces):
        piece = term[i * group : (i + 1) * group]
        for way in (0, 1):
            full_copies[way][0][i].wait_recv()
            piece = piece + full_in[way, 0, rows, :].astype(F32)
        row_out[rows, :] = piece.astype(BF)
        start(row_copies[i])
    term = share(0, 1)
    for i, rows in enumerate(pieces):
        row_copies[i].wait_recv()
        piece = term[i * group : (i + 1) * group] + row_in[rows, :].astype(F32)
        for way in (0, 1):
            full_copies[way][1][i].wait_recv()
            piece = piece + full_in[way, 1, rows, :].astype(F32)
        gin_ref[rows, :] = piece.astype(BF)

    for copy in sent:
        copy.wait_send()


def hand_on(a_ref, b_ref, a_out, b_out, a_held, b_held, sems):
    arrive = [pltpu.make_async_copy(a_ref, a_held, sems.at[0]), pltpu.make_async_copy(b_ref, b_held, sems.at[1])]
    leave = [pltpu.make_async_copy(a_held, a_out, sems.at[2]), pltpu.make_async_copy(b_held, b_out, sems.at[3])]
    for copy in arrive:
        copy.start()
    for copy, following in zip(arrive, leave):
        copy.wait()
        following.start()
    for copy in leave:
        copy.wait()


def on_device(activations, qkv_weight, grad_out):
    length, depth = activations.shape
    width = grad_out.shape[1]
    half = length // 2
    steps = lax.axis_size("seq") // 8
    weights = jnp.transpose(qkv_weight, (1, 0, 2))
    anywhere = pl.BlockSpec(memory_space=pl.ANY)
    vmem = pl.BlockSpec(memory_space=pltpu.VMEM)
    dma = pltpu.SemaphoreType.DMA
    attention, grad_input = pl.pallas_call(
        kernel,
        out_shape=(
            jax.ShapeDtypeStruct((length, width), BF),
            jax.ShapeDtypeStruct((half, depth), BF),
        ),
        in_specs=[anywhere] * 3,
        out_specs=(vmem, vmem),
        scratch_shapes=[
            pltpu.VMEM((4, length, depth), BF),
            pltpu.VMEM((4, depth, 3 * width), BF),
            pltpu.VMEM((length, 3 * width), F32),
            pltpu.VMEM((HEADS, length, HEAD), BF),
            pltpu.VMEM((HEADS, HEAD, length), BF),
            pltpu.VMEM((HEADS, length, HEAD), BF),
            pltpu.VMEM((HEADS, 2, length, HEAD), BF),
            pltpu.VMEM((HEADS, 2, HEAD, length), BF),
            pltpu.VMEM((HEADS, 2, length, HEAD), BF),
            pltpu.VMEM((HEADS, 2, HEAD, length), BF),
            pltpu.VMEM((HEADS, 2, length), F32),
            *[pltpu.VMEM((HEADS, *tile), kind) for kind in (F32, F32, BF, BF) for tile in TILES],
            pltpu.VMEM((length, length), BF),
            pltpu.VMEM((HEADS, length, length), BF),
            pltpu.VMEM((HEADS, 2, length, HEAD), F32),
            pltpu.VMEM((HEADS, 2, length, HEAD), BF),
            pltpu.VMEM((HEADS, 2, length, HEAD), BF),
            pltpu.VMEM((length, 3 * width), BF),
            pltpu.VMEM((half, depth), BF),
            pltpu.VMEM((half, depth), BF),
            pltpu.VMEM((2, half, depth // 2), BF),
            pltpu.VMEM((2, half, depth // 2), BF),
            pltpu.VMEM((2, 2, half, depth), BF),
            pltpu.VMEM((2, 2, half, depth), BF),
            pltpu.VMEM((half, depth), BF),
            pltpu.VMEM((half, depth), BF),
            dma((7,)),
            *[dma((15,))] * 2,
            *[dma((2, 3))] * 2,
            *[dma((2,))] * 4,
            *[dma((2, steps, 2))] * 2,
            *[dma((2, 2 * steps))] * 2,
            *[dma((HEADS + 1,))] * 2,
            *[dma((HEADS - 1 + GROUPS,))] * 2,
            *[dma((GROUPS // 2,))] * 2,
            *[dma((2, GROUPS // 2))] * 2,
            *[dma((2, 2, GROUPS // 2))] * 2,
            *[dma((GROUPS // 2,))] * 2,
        ],
        compiler_params=pltpu.CompilerParams(
            collective_id=0, has_side_effects=True, vmem_limit_bytes=60 * 2**20
        ),
    )(activations, weights, grad_out)
    return pl.pallas_call(
        hand_on,
        out_shape=(
            jax.ShapeDtypeStruct((length, width), BF),
            jax.ShapeDtypeStruct((half, depth), BF),
        ),
        in_specs=[anywhere] * 2,
        out_specs=(anywhere, anywhere),
        scratch_shapes=[pltpu.VMEM((length, width), BF), pltpu.VMEM((half, depth), BF), dma((4,))],
        compiler_params=pltpu.CompilerParams(vmem_limit_bytes=60 * 2**20),
    )(attention, grad_input)


def solution(mesh):
    in_specs = (P("seq", "col"), P("col", None, "row"), P("seq", ("row", "col")))
    out_specs = (P("seq", ("row", "col")), P(("seq", "row"), "col"))
    return jax.shard_map(on_device, mesh=mesh, in_specs=in_specs, out_specs=out_specs, check_vma=False)
```
